512 devices in a mesh: samp: 32 (over y, x, core), kmer: 16 (over z).
Axes of the slice: x: 4, y: 4, z: 16, core: 2. Of those that a mesh axis runs over, the one named last changes fastest.
Arguments:
- tile_rows: int32 [32, 16, 32], P('samp', 'kmer'), may hold values from 0 to 3, as said below
- tile_cols: int32 [32, 16, 32], P('samp', 'kmer'), may hold values from 0 to 31
- tile_count: int32 [32, 16], P('samp', 'kmer'), may hold values from 4 to 32, as said below
- tile_values: bfloat16 [32, 16, 32, 128, 128], P('samp', 'kmer'), may hold values from 0.049804688 to 20
- w_init: float32 [16384, 64], P(('samp', 'kmer')), may hold values from 0.1 to 30, as said below
- h_init: float32 [64, 65536], P(None, ('kmer', 'samp')), may hold values from 0.1 to 30, as said below
Outputs:
- w_final: float32 [16384, 64], P(('samp', 'kmer'))
- h_final: float32 [64, 65536], P(None, ('kmer', 'samp'))
The draws below stay inside these ranges and needn't reach their ends.
Inputs may be any that keep to these rules, and one draw needn't show every extreme that they name: Within a device all 32 slots hold distinct (tile_rows, tile_cols) pairs. `tile_count`: some device has all 32 slots live in every draw. `w_init`: Positive. `h_init`: Positive.
All inputs are finite; a program needn't handle non-finite values.
Results may differ from the reference program's by a relative error of at most 0.00051.
Values may be sent and summed in bfloat16 or wider, within the bound.
No kernel may reach another device: no remote copies, remote signals or barrier semaphores. Data moves between devices by JAX's collectives and lax.ppermute only.
A program may use at most 64 MiB of HBM per device.

```python
import math
import jax
import jax.numpy as jnp
from jax import lax

TILE = 128
RANK = 64
ROW_TILES = 4
COL_TILES = 32
CAP = 32
ITERS = 2
SAMPLES = 16384
KMERS = 65536
N_SAMP = 32
N_KMER = 16


def tile_slots(key):
    key_list = jax.random.split(key, N_SAMP * N_KMER)
    orders = jax.vmap(lambda subkey: jax.random.permutation(subkey, ROW_TILES * COL_TILES)[:CAP])(key_list)
    return orders.reshape(N_SAMP, N_KMER, CAP).astype(jnp.int32)


def draw_tile_rows(key, part):
    slots = tile_slots(key)
    return (slots // COL_TILES).astype(jnp.int32)


def draw_tile_cols(key, part):
    slots = tile_slots(key)
    return (slots % COL_TILES).astype(jnp.int32)


def draw_tile_count(key, part):
    key = jax.random.fold_in(key, 3)
    first_key, second_key = jax.random.split(key)
    base = jax.random.randint(first_key, (N_SAMP * N_KMER,), max(1, CAP // 8), CAP // 2 + 1)
    picked = jax.random.randint(second_key, (4,), 0, N_SAMP * N_KMER)
    hits = jnp.any(jnp.arange(N_SAMP * N_KMER)[:, None] == picked[None, :], axis=1)
    return jnp.where(hits, CAP, base).reshape(N_SAMP, N_KMER).astype(jnp.int32)


def draw_w_init(key, part):
    key = jax.random.fold_in(key, 5)
    first_key = jax.random.fold_in(key, 0)
    rising = 1.0 + 2.0 * jnp.arange(SAMPLES, dtype=jnp.float32)[:, None] / SAMPLES
    base = jnp.exp(jax.random.uniform(first_key, (SAMPLES, RANK), jnp.float32, -1.6, 0.7))
    return base * rising


def draw_h_init(key, part):
    key = jax.random.fold_in(key, 7)
    first_key = jax.random.fold_in(key, 0)
    rising = 1.0 + 2.0 * jnp.arange(KMERS, dtype=jnp.float32)[None, :] / KMERS
    base = jnp.exp(jax.random.uniform(first_key, (RANK, KMERS), jnp.float32, -1.6, 0.7))
    return base * rising


def block_levels(own_key, dims, cuts, low, high):
    def one(position, shards_of):
        draws = jax.random.uniform(jax.random.fold_in(jax.random.fold_in(own_key, 6), position), (shards_of,), jnp.float32, low / len(cuts), high / len(cuts))
        return jnp.repeat(jnp.exp(draws), dims[position] // shards_of).reshape((-1,) + (1,) * (len(dims) - position - 1))

    level = one(*cuts[0])
    for cut in cuts[1:]:
        level = level * one(*cut)
    return level


def setup_inputs(seed: int = 0) -> dict:
    seeds = jax.random.split(jax.random.key(seed), 7)
    return {
        "tile_rows": draw_tile_rows(jax.random.fold_in(seeds[6], 71), 0),
        "tile_cols": draw_tile_cols(jax.random.fold_in(seeds[6], 71), 0),
        "tile_count": draw_tile_count(jax.random.fold_in(seeds[6], 71), 0),
        "tile_values": jnp.clip(jnp.exp(math.log(20.0) - 5.9953784 * jax.random.uniform(seeds[3], (N_SAMP, N_KMER, CAP, TILE, TILE), jnp.float32) ** block_levels(seeds[3], (N_SAMP, N_KMER, CAP, TILE, TILE), ((0, 32), (1, 16)), -0.2, 0.2)), 0.049804688, 20.0).astype(jnp.bfloat16),
        "w_init": draw_w_init(jax.random.fold_in(seeds[6], 71), 0),
        "h_init": draw_h_init(jax.random.fold_in(seeds[6], 71), 0),
    }


def tile_terms(w_table, h_table, rows_here, cols_here, values_here, live_here):
    w_tiles = w_table[rows_here].astype(jnp.float32)
    h_tiles = h_table[cols_here].astype(jnp.float32)
    estimate = jnp.einsum("gik,gkj->gij", w_tiles, h_tiles)
    ratio = jnp.where(live_here[:, None, None], values_here.astype(jnp.float32) / estimate, 0.0)
    ratio = lax.optimization_barrier(ratio.astype(jnp.bfloat16))
    return w_tiles, h_tiles, ratio.astype(jnp.float32)


def reference(tile_rows, tile_cols, tile_count, tile_values, w_init, h_init):
    live = jnp.arange(CAP, dtype=jnp.int32)[None, None, :] < tile_count[:, :, None]
    global_rows = jnp.arange(N_SAMP, dtype=jnp.int32)[:, None, None] * ROW_TILES + tile_rows
    global_cols = jnp.arange(N_KMER, dtype=jnp.int32)[None, :, None] * COL_TILES + tile_cols
    global_rows = global_rows.astype(jnp.int32)
    global_cols = jnp.broadcast_to(global_cols, tile_rows.shape).astype(jnp.int32)
    w_full = w_init
    h_full = h_init
    for sweep_index in range(ITERS):
        w_half = w_full.astype(jnp.bfloat16)
        h_half = h_full.astype(jnp.bfloat16)
        col_total = jnp.sum(w_half.astype(jnp.float32), axis=0)
        w_table = w_half.reshape(-1, TILE, RANK)
        h_table = jnp.transpose(h_half.reshape(RANK, -1, TILE), (1, 0, 2))

        def h_step(running, device_row):
            rows_here, cols_here, values_here, live_here = device_row
            flat_cols = cols_here.reshape(-1)
            w_tiles, h_tiles, ratio = tile_terms(w_table, h_table, rows_here.reshape(-1), flat_cols, values_here.reshape(-1, TILE, TILE), live_here.reshape(-1))
            contribution = jnp.einsum("gik,gij->gkj", w_tiles, ratio)
            return running + jax.ops.segment_sum(contribution, flat_cols, num_segments=KMERS // TILE), None

        start = jnp.zeros((KMERS // TILE, RANK, TILE), jnp.float32)
        numer_h, ignored = lax.scan(h_step, start, (global_rows, global_cols, tile_values, live))
        numer_h = jnp.transpose(numer_h, (1, 0, 2)).reshape(RANK, KMERS)
        h_full = h_full * numer_h / col_total[:, None]
        h_half = h_full.astype(jnp.bfloat16)
        row_total = jnp.sum(h_half.astype(jnp.float32), axis=1)
        h_table = jnp.transpose(h_half.reshape(RANK, -1, TILE), (1, 0, 2))

        def w_step(device_row):
            rows_here, cols_here, local_rows, values_here, live_here = device_row
            w_tiles, h_tiles, ratio = tile_terms(w_table, h_table, rows_here.reshape(-1), cols_here.reshape(-1), values_here.reshape(-1, TILE, TILE), live_here.reshape(-1))
            contribution = jnp.einsum("gij,gkj->gik", ratio, h_tiles)
            return jax.ops.segment_sum(contribution, local_rows.reshape(-1), num_segments=ROW_TILES)

        numer_w = lax.map(w_step, (global_rows, global_cols, tile_rows, tile_values, live))
        numer_w = numer_w.reshape(SAMPLES, RANK)
        w_full = w_full * numer_w / row_total[None, :]
    return w_full, h_full
```

```python
import jax
import jax.numpy as jnp
from jax import lax
from jax.sharding import PartitionSpec as P

ROW_TILES = 4
COL_TILES = 32
ITERS = 2
N_SAMP = 32
N_KMER = 16


def spread(x, axis_name, size):
    return lax.all_to_all(jnp.broadcast_to(x[None], (size,) + x.shape), axis_name, 0, 0)


def tile_ratio(w_tiles, h_tiles, values, live_slots):
    estimate = jnp.einsum("gik,gkj->gij", w_tiles, h_tiles, preferred_element_type=jnp.float32)
    ratio = jnp.where(live_slots[:, None, None], values.astype(jnp.float32) / estimate, 0.0)
    return ratio.astype(jnp.bfloat16)


def body(tile_rows, tile_cols, tile_count, tile_values, w_init, h_init):
    tile_size = tile_values.shape[-1]
    rank_size = w_init.shape[1]
    values = tile_values.reshape(-1, tile_size, tile_size)
    row_index = tile_rows.reshape(-1)
    col_index = tile_cols.reshape(-1)
    live_slots = jnp.arange(row_index.shape[0], dtype=jnp.int32) < tile_count.reshape(())
    col_hot = (col_index[:, None] == jnp.arange(COL_TILES, dtype=jnp.int32)[None, :]).astype(
        jnp.float32
    )
    row_hot = (row_index[:, None] == jnp.arange(ROW_TILES, dtype=jnp.int32)[None, :]).astype(
        jnp.float32
    )
    w_own = w_init
    h_own = h_init
    h_panel = spread(h_own.astype(jnp.bfloat16), "samp", N_SAMP)
    for sweep_index in range(ITERS):
        w_panel = spread(w_own.astype(jnp.bfloat16), "kmer", N_KMER)
        w_panel = w_panel.reshape(ROW_TILES, tile_size, rank_size)
        w_tiles = jnp.take(w_panel, row_index, axis=0)
        col_part = jnp.sum(w_panel.astype(jnp.float32), axis=(0, 1))
        h_tiles = jnp.take(h_panel, col_index, axis=0)
        ratio = tile_ratio(w_tiles, h_tiles, values, live_slots)
        contribution = jnp.einsum(
            "gik,gij->gkj", w_tiles, ratio, preferred_element_type=jnp.float32
        )
        numerator = jnp.einsum(
            "gc,gkj->ckj", col_hot, contribution, precision=lax.Precision.HIGHEST
        )
        col_row = jnp.pad(col_part, (0, tile_size - rank_size))
        col_rows = jnp.broadcast_to(col_row[None, None, :], (COL_TILES, 8, tile_size))
        parts = lax.all_to_all(jnp.concatenate([numerator, col_rows], axis=1), "samp", 0, 0)
        summed = jnp.sum(parts, axis=0)
        col_total = summed[rank_size, :rank_size]
        h_own = h_own * summed[:rank_size] / col_total[:, None]
        h_panel = spread(h_own.astype(jnp.bfloat16), "samp", N_SAMP)
        row_part = jnp.sum(h_panel.astype(jnp.float32), axis=(0, 2))
        h_tiles = jnp.take(h_panel, col_index, axis=0)
        ratio = tile_ratio(w_tiles, h_tiles, values, live_slots)
        contribution = jnp.einsum(
            "gij,gkj->gik", ratio, h_tiles, preferred_element_type=jnp.float32
        )
        numerator = jnp.einsum(
            "gr,gik->rik", row_hot, contribution, precision=lax.Precision.HIGHEST
        )
        numerator = numerator.reshape(N_KMER, -1, rank_size)
        row_rows = jnp.broadcast_to(row_part[None, None, :], (N_KMER, 8, rank_size))
        parts = lax.all_to_all(jnp.concatenate([numerator, row_rows], axis=1), "kmer", 0, 0)
        summed = jnp.sum(parts, axis=0)
        own_rows = w_own.shape[0]
        w_own = w_own * summed[:own_rows] / summed[own_rows][None, :]
    return (w_own, h_own)


def solution(mesh):
    in_specs = (
        P("samp", "kmer", None),
        P("samp", "kmer", None),
        P("samp", "kmer"),
        P("samp", "kmer", None, None, None),
        P(("samp", "kmer"), None),
        P(None, ("kmer", "samp")),
    )
    out_specs = (P(("samp", "kmer"), None), P(None, ("kmer", "samp")))
    return jax.shard_map(body, mesh=mesh, in_specs=in_specs, out_specs=out_specs, check_vma=False)
```

```python
import functools

import jax
import jax.numpy as jnp
from jax import lax
from jax.experimental import pallas as pl
from jax.experimental.pallas import tpu as pltpu
from jax.sharding import PartitionSpec as P

TILE = 128
RANK = 64
ROW_TILES = 4
COL_TILES = 32
CAP = 32
ITERS = 2
N_KMER = 16
N_CHIP = 16
OWN = 16
SUMS = 8

CORES = [[2 * a, 2 * a + 1] for a in range(N_CHIP)]
CHIPS = [[2 * a + c for a in range(N_CHIP)] for c in range(2)]

f32 = jnp.float32
bf16 = jnp.bfloat16
VMEM = pl.BlockSpec(memory_space=pltpu.VMEM)
SMEM = pl.BlockSpec(memory_space=pltpu.SMEM)


def call(kernel, out_shape, in_specs, scratch=(), flops=0):
    return pl.pallas_call(
        kernel,
        out_shape=out_shape,
        in_specs=in_specs,
        out_specs=jax.tree.map(lambda _: VMEM, out_shape),
        scratch_shapes=scratch,
        compiler_params=pltpu.CompilerParams(vmem_limit_bytes=32 * 2**20),
    )


def same_rank(shape):
    rank = lax.broadcasted_iota(jnp.int32, shape, 0)
    lane = lax.broadcasted_iota(jnp.int32, shape, 1)
    return jnp.bitwise_and(lane, RANK - 1) == rank


def start_kernel(w_ref, h_ref, own_ref, w_out, h_out):
    own_ref[:, :RANK] = w_ref[:OWN, :]
    own_ref[:, RANK:] = w_ref[OWN:, :]
    half = own_ref[...].astype(bf16)
    for k in range(N_KMER):
        w_out[k] = half
    h_half = h_ref[...].astype(bf16)
    for k in range(N_CHIP):
        h_out[k] = h_half


def unpack(w_ref, tiles_ref):
    for k in range(N_KMER):
        r, q = k // 4, k % 4
        block = w_ref[k]
        tiles_ref[r, 32 * q : 32 * q + OWN, :] = block[:, :RANK]
        tiles_ref[r, 32 * q + OWN : 32 * q + 2 * OWN, :] = block[:, RANK:]


def ratio_of(g, rows, cols, count, values_ref, tiles_ref, h_ref):
    r, c = rows[g], cols[g]
    h_tile = h_ref[c & 1, c >> 1]
    estimate = jnp.dot(tiles_ref[r], h_tile, preferred_element_type=f32)
    ratio = values_ref[g].astype(f32) / estimate
    ratio = jnp.where(g < count[0], ratio, 0.0).astype(bf16)
    return r, c, h_tile, ratio


def numer_h_kernel(rows, cols, count, values_ref, w_ref, h_ref, out_ref, tiles_ref, flip_ref):
    unpack(w_ref, tiles_ref)
    for r in range(ROW_TILES):
        flip_ref[r] = tiles_ref[r].T
    sums = jnp.sum(w_ref[...].astype(f32).reshape(N_KMER * OWN, 2 * RANK), axis=0, keepdims=True)
    out_ref[:, :, :RANK, :] = jnp.zeros((2, N_CHIP, RANK, TILE), f32)
    out_ref[:, :, RANK:, :] = jnp.broadcast_to(sums[None, None], (2, N_CHIP, SUMS, TILE))
    for g in range(CAP):
        r, c, h_tile, ratio = ratio_of(g, rows, cols, count, values_ref, tiles_ref, h_ref)
        out_ref[c & 1, c >> 1, :RANK, :] += jnp.dot(flip_ref[r], ratio, preferred_element_type=f32)


def update_h_kernel(parts_ref, h_ref, own_ref, out_ref):
    summed = parts_ref[0]
    for k in range(1, N_CHIP):
        summed = summed + parts_ref[k]
    total = jnp.where(same_rank((RANK, TILE)), summed[RANK : RANK + 1], 0.0)
    h_new = h_ref[...] * summed[:RANK] / jnp.sum(total, axis=1, keepdims=True)
    own_ref[...] = h_new
    half = h_new.astype(bf16)
    for k in range(N_CHIP):
        out_ref[k] = half


def numer_w_kernel(rows, cols, count, values_ref, w_ref, h_ref, out_ref, tiles_ref, acc_ref):
    unpack(w_ref, tiles_ref)
    sums = jnp.zeros((RANK, TILE), f32)
    for c in range(COL_TILES):
        sums = sums + h_ref[c % 2, c // 2].astype(f32)
    sums = jnp.where(same_rank((RANK, TILE)), jnp.sum(sums, axis=1, keepdims=True), 0.0)
    sums = jnp.sum(sums, axis=0, keepdims=True)
    out_ref[:, OWN:, :] = jnp.broadcast_to(sums[None], (N_KMER, SUMS, TILE))
    acc_ref[...] = jnp.zeros_like(acc_ref)
    for g in range(CAP):
        r, c, h_tile, ratio = ratio_of(g, rows, cols, count, values_ref, tiles_ref, h_ref)
        acc_ref[r] += lax.dot_general(
            ratio, h_tile, (((1,), (1,)), ((), ())), preferred_element_type=f32
        )
    for k in range(N_KMER):
        r, q = k // 4, k % 4
        out_ref[k, :OWN, :RANK] = acc_ref[r, 32 * q : 32 * q + OWN, :]
        out_ref[k, :OWN, RANK:] = acc_ref[r, 32 * q + OWN : 32 * q + 2 * OWN, :]


def new_w(parts_ref, w_ref):
    summed = parts_ref[0]
    for k in range(1, N_KMER):
        summed = summed + parts_ref[k]
    return w_ref[...] * summed[:OWN] / summed[OWN : OWN + 1]


def update_w_kernel(parts_ref, w_ref, own_ref, out_ref):
    w_new = new_w(parts_ref, w_ref)
    own_ref[...] = w_new
    half = w_new.astype(bf16)
    for k in range(N_KMER):
        out_ref[k] = half


def last_w_kernel(parts_ref, w_ref, own_ref):
    w_new = new_w(parts_ref, w_ref)
    own_ref[:OWN, :] = w_new[:, :RANK]
    own_ref[OWN:, :] = w_new[:, RANK:]


def to_kmer(x):
    return lax.all_to_all(x, "kmer", 0, 0)


def to_chips(x):
    return lax.all_to_all(x, "samp", 0, 0, axis_index_groups=CHIPS)


def panel_of(spread):
    return lax.all_gather(to_chips(spread), "samp", axis=0, axis_index_groups=CORES)


def body(tile_rows, tile_cols, tile_count, tile_values, w_init, h_init):
    shape = jax.ShapeDtypeStruct
    slots = (tile_rows.reshape(-1), tile_cols.reshape(-1), tile_count.reshape(-1))
    values = tile_values.reshape(CAP, TILE, TILE)
    w_spread = shape((N_KMER, OWN, 2 * RANK), bf16)
    h_spread = shape((N_CHIP, RANK, TILE), bf16)
    w_own, h_own = shape((OWN, 2 * RANK), f32), shape((RANK, TILE), f32)
    tiles = pltpu.VMEM((ROW_TILES, TILE, RANK), bf16)
    flip = pltpu.VMEM((ROW_TILES, RANK, TILE), bf16)
    acc = pltpu.VMEM((ROW_TILES, TILE, RANK), f32)
    wide = [SMEM] * 3 + [VMEM] * 3

    start = call(start_kernel, (w_own, w_spread, h_spread), [VMEM] * 2)
    numer_h = call(numer_h_kernel, shape((2, N_CHIP, RANK + SUMS, TILE), f32), wide, [tiles, flip])
    update_h = call(update_h_kernel, (h_own, h_spread), [VMEM] * 2)
    numer_w = call(numer_w_kernel, shape((N_KMER, OWN + SUMS, TILE), f32), wide, [tiles, acc])
    update_w = call(update_w_kernel, (w_own, w_spread), [VMEM] * 2)
    last_w = call(last_w_kernel, shape((2 * OWN, RANK), f32), [VMEM] * 2)

    w_own, w_out, h_out = start(w_init, h_init)
    h_own = h_init
    w_panel = to_kmer(w_out)
    w_panel, h_out = lax.optimization_barrier((w_panel, h_out))
    h_panel = panel_of(h_out)
    for sweep in range(ITERS):
        numer = numer_h(*slots, values, w_panel, h_panel)
        halves = lax.all_to_all(numer, "samp", 0, 0, axis_index_groups=CORES)
        h_own, h_out = update_h(to_chips(halves[0] + halves[1]), h_own)
        h_panel = panel_of(h_out)
        parts = to_kmer(numer_w(*slots, values, w_panel, h_panel))
        if sweep < ITERS - 1:
            w_own, w_out = update_w(parts, w_own)
            w_panel = to_kmer(w_out)
    return last_w(parts, w_own), h_own


def solution(mesh):
    in_specs = (
        P("samp", "kmer", None),
        P("samp", "kmer", None),
        P("samp", "kmer"),
        P("samp", "kmer", None, None, None),
        P(("samp", "kmer"), None),
        P(None, ("kmer", "samp")),
    )
    out_specs = (P(("samp", "kmer"), None), P(None, ("kmer", "samp")))
    return jax.shard_map(body, mesh=mesh, in_specs=in_specs, out_specs=out_specs, check_vma=False)
```

```python
import functools

import jax
import jax.numpy as jnp
from jax import lax
from jax.experimental import pallas as pl
from jax.experimental.pallas import tpu as pltpu
from jax.sharding import PartitionSpec as P

TILE = 128
RANK = 64
ROW_TILES = 4
COL_TILES = 32
CAP = 32
ITERS = 2
N_KMER = 16
N_CHIP = 16
OWN = 16
SUMS = 8
QUAD = 4
QUADS = OWN // QUAD + 1

CORES = [[2 * a, 2 * a + 1] for a in range(N_CHIP)]
CHIPS = [[2 * a + c for a in range(N_CHIP)] for c in range(2)]

f32 = jnp.float32
bf16 = jnp.bfloat16
VMEM = pl.BlockSpec(memory_space=pltpu.VMEM)
SMEM = pl.BlockSpec(memory_space=pltpu.SMEM)
HBM = pl.BlockSpec(memory_space=pltpu.HBM)


def call(kernel, out_shape, in_specs, scratch=()):
    return pl.pallas_call(
        kernel,
        out_shape=out_shape,
        in_specs=in_specs,
        out_specs=jax.tree.map(lambda _: VMEM, out_shape),
        scratch_shapes=scratch,
        compiler_params=pltpu.CompilerParams(vmem_limit_bytes=32 * 2**20),
    )


def same_rank(shape):
    rank = lax.broadcasted_iota(jnp.int32, shape, 0)
    lane = lax.broadcasted_iota(jnp.int32, shape, 1)
    return jnp.bitwise_and(lane, RANK - 1) == rank


def start_kernel(count, w_any, h_any, own_ref, w_out, h_out, live_ref, w_ref, h_ref, sems):
    w_copy = pltpu.make_async_copy(w_any, w_ref, sems.at[0])
    h_copy = pltpu.make_async_copy(h_any, h_ref, sems.at[1])
    w_copy.start()
    h_copy.start()
    slot = lax.broadcasted_iota(jnp.int32, (CAP, TILE), 0)
    live_ref[...] = (slot < count[0, 0]).astype(f32)
    w_copy.wait()
    own_ref[:, :RANK] = w_ref[:OWN, :]
    own_ref[:, RANK:] = w_ref[OWN:, :]
    half = own_ref[...].astype(bf16)
    for k in range(N_KMER):
        w_out[k] = half
    h_copy.wait()
    h_half = h_ref[...].astype(bf16)
    for k in range(N_CHIP):
        h_out[k] = h_half


def unpack(w_ref, tiles_ref):
    for k in range(N_KMER):
        r, q = k // 4, k % 4
        block = w_ref[k]
        tiles_ref[r, 32 * q : 32 * q + OWN, :] = block[:, :RANK]
        tiles_ref[r, 32 * q + OWN : 32 * q + 2 * OWN, :] = block[:, RANK:]


def ratio_of(g, rows, cols, live_ref, values_ref, tiles_ref, h_ref):
    r, c = rows[0, 0, g], cols[0, 0, g]
    h_tile = h_ref[c & 1, c >> 1]
    estimate = jnp.dot(tiles_ref[r], h_tile, preferred_element_type=f32)
    ratio = values_ref[g].astype(f32) / estimate
    ratio = jnp.where(live_ref[g : g + 1, :] > 0.0, ratio, 0.0).astype(bf16)
    return r, c, h_tile, ratio


def numer_h_kernel(rows, cols, live_ref, values_ref, w_ref, h_ref, out_ref, tiles_ref, flip_ref):
    unpack(w_ref, tiles_ref)
    for r in range(ROW_TILES):
        flip_ref[r] = tiles_ref[r].T
    sums = jnp.sum(w_ref[...].astype(f32).reshape(N_KMER * OWN, 2 * RANK), axis=0, keepdims=True)
    out_ref[:, :, :RANK, :] = jnp.zeros((2, N_CHIP, RANK, TILE), f32)
    out_ref[:, :, RANK:, :] = jnp.broadcast_to(sums[None, None], (2, N_CHIP, SUMS, TILE))
    for g in range(CAP):
        r, c, h_tile, ratio = ratio_of(g, rows, cols, live_ref, values_ref, tiles_ref, h_ref)
        out_ref[c & 1, c >> 1, :RANK, :] += jnp.dot(flip_ref[r], ratio, preferred_element_type=f32)


def update_h_kernel(parts_ref, h_ref, own_ref, out_ref):
    summed = parts_ref[0]
    for k in range(1, N_CHIP):
        summed = summed + parts_ref[k]
    total = jnp.where(same_rank((RANK, TILE)), summed[RANK : RANK + 1], 0.0)
    h_new = h_ref[...] * summed[:RANK] / jnp.sum(total, axis=1, keepdims=True)
    own_ref[...] = h_new
    half = h_new.astype(bf16)
    for k in range(N_CHIP):
        out_ref[k] = half


def numer_w_kernel(rows, cols, live_ref, values_ref, w_ref, h_ref, out_ref, tiles_ref, acc_ref):
    unpack(w_ref, tiles_ref)
    sums = jnp.zeros((RANK, TILE), f32)
    for c in range(COL_TILES):
        sums = sums + h_ref[c % 2, c // 2].astype(f32)
    sums = jnp.where(same_rank((RANK, TILE)), jnp.sum(sums, axis=1, keepdims=True), 0.0)
    sums = jnp.sum(sums, axis=0, keepdims=True)
    out_ref[:, QUADS - 1] = jnp.broadcast_to(sums[None], (N_KMER, QUAD, TILE))
    acc_ref[...] = jnp.zeros_like(acc_ref)
    for g in range(CAP):
        r, c, h_tile, ratio = ratio_of(g, rows, cols, live_ref, values_ref, tiles_ref, h_ref)
        acc_ref[r] += lax.dot_general(
            ratio, h_tile, (((1,), (1,)), ((), ())), preferred_element_type=f32
        )
    for k in range(N_KMER):
        r, q = k // 4, k % 4
        for a in range(OWN // QUAD):
            row = 32 * q + QUAD * a
            out_ref[k, a, :, :RANK] = acc_ref[r, row : row + QUAD, :]
            out_ref[k, a, :, RANK:] = acc_ref[r, row + OWN : row + OWN + QUAD, :]


def new_w(parts_ref, w_ref, rows_ref):
    summed = parts_ref[0]
    for k in range(1, N_KMER):
        summed = summed + parts_ref[k]
    for a in range(OWN // QUAD):
        rows_ref[QUAD * a : QUAD * a + QUAD, :] = summed[a]
    return w_ref[...] * rows_ref[...] / summed[QUADS - 1, :1]


def update_w_kernel(parts_ref, w_ref, own_ref, out_ref, rows_ref):
    w_new = new_w(parts_ref, w_ref, rows_ref)
    own_ref[...] = w_new
    half = w_new.astype(bf16)
    for k in range(N_KMER):
        out_ref[k] = half


def last_w_kernel(parts_ref, w_ref, own_ref, rows_ref):
    w_new = new_w(parts_ref, w_ref, rows_ref)
    own_ref[:OWN, :] = w_new[:, :RANK]
    own_ref[OWN:, :] = w_new[:, RANK:]


def to_kmer(x):
    return lax.all_to_all(x, "kmer", 0, 0)


def to_chips(x):
    return lax.all_to_all(x, "samp", 0, 0, axis_index_groups=CHIPS)


def panel_of(spread):
    return lax.all_gather(to_chips(spread), "samp", axis=0, axis_index_groups=CORES)


def body(tile_rows, tile_cols, tile_count, tile_values, w_init, h_init):
    shape = jax.ShapeDtypeStruct
    values = tile_values.reshape(CAP, TILE, TILE)
    w_spread = shape((N_KMER, OWN, 2 * RANK), bf16)
    h_spread = shape((N_CHIP, RANK, TILE), bf16)
    w_own, h_own = shape((OWN, 2 * RANK), f32), shape((RANK, TILE), f32)
    tiles = pltpu.VMEM((ROW_TILES, TILE, RANK), bf16)
    flip = pltpu.VMEM((ROW_TILES, RANK, TILE), bf16)
    acc = pltpu.VMEM((ROW_TILES, TILE, RANK), f32)
    rows = pltpu.VMEM((OWN, 2 * RANK), f32)
    fetched = [pltpu.VMEM(w_init.shape, f32), pltpu.VMEM(h_init.shape, f32), pltpu.SemaphoreType.DMA((2,))]
    wide = [SMEM] * 2 + [VMEM] * 4

    live = shape((CAP, TILE), f32)
    start = call(start_kernel, (w_own, w_spread, h_spread, live), [SMEM] + [HBM] * 2, fetched)
    numer_h = call(numer_h_kernel, shape((2, N_CHIP, RANK + SUMS, TILE), f32), wide, [tiles, flip])
    update_h = call(update_h_kernel, (h_own, h_spread), [VMEM] * 2)
    numer_w = call(numer_w_kernel, shape((N_KMER, QUADS, QUAD, TILE), f32), wide, [tiles, acc])
    update_w = call(update_w_kernel, (w_own, w_spread), [VMEM] * 2, [rows])
    last_w = call(last_w_kernel, shape((2 * OWN, RANK), f32), [VMEM] * 2, [rows])

    w_own, w_out, h_out, live = start(tile_count, w_init, h_init)
    slots = (tile_rows, tile_cols, live)
    h_own = h_init
    w_panel = to_kmer(w_out)
    w_panel, h_out = lax.optimization_barrier((w_panel, h_out))
    h_panel = panel_of(h_out)
    for sweep in range(ITERS):
        numer = numer_h(*slots, values, w_panel, h_panel)
        halves = lax.all_to_all(numer, "samp", 0, 0, axis_index_groups=CORES)
        h_own, h_out = update_h(to_chips(halves[0] + halves[1]), h_own)
        h_panel = panel_of(h_out)
        parts = to_kmer(numer_w(*slots, values, w_panel, h_panel))
        if sweep < ITERS - 1:
            w_own, w_out = update_w(parts, w_own)
            w_panel = to_kmer(w_out)
    return last_w(parts, w_own), h_own


def solution(mesh):
    in_specs = (
        P("samp", "kmer", None),
        P("samp", "kmer", None),
        P("samp", "kmer"),
        P("samp", "kmer", None, None, None),
        P(("samp", "kmer"), None),
        P(None, ("kmer", "samp")),
    )
    out_specs = (P(("samp", "kmer"), None), P(None, ("kmer", "samp")))
    return jax.shard_map(body, mesh=mesh, in_specs=in_specs, out_specs=out_specs, check_vma=False)
```

```python
import jax
import jax.numpy as jnp
from jax import lax
from jax.experimental import pallas as pl
from jax.experimental.pallas import tpu as pltpu
from jax.sharding import PartitionSpec as P

TILE = 128
RANK = 64
ROW_TILES = 4
COL_TILES = 32
CAP = 32
ITERS = 2
N_KMER = 16
N_CHIP = 16
OWN = 16
SUMS = 8
QUAD = 4
QUADS = OWN // QUAD + 1

CORES = [[2 * a, 2 * a + 1] for a in range(N_CHIP)]
CHIPS = [[2 * a + c for a in range(N_CHIP)] for c in range(2)]

f32 = jnp.float32
bf16 = jnp.bfloat16
VMEM = pl.BlockSpec(memory_space=pltpu.VMEM)
SMEM = pl.BlockSpec(memory_space=pltpu.SMEM)


def call(kernel, out_shape, in_specs, scratch=()):
    return pl.pallas_call(
        kernel,
        out_shape=out_shape,
        in_specs=in_specs,
        out_specs=jax.tree.map(lambda x: SMEM if x.dtype == jnp.int32 else VMEM, out_shape),
        scratch_shapes=scratch,
        compiler_params=pltpu.CompilerParams(vmem_limit_bytes=32 * 2**20),
    )


def same_rank(shape):
    rank = lax.broadcasted_iota(jnp.int32, shape, 0)
    lane = lax.broadcasted_iota(jnp.int32, shape, 1)
    return jnp.bitwise_and(lane, RANK - 1) == rank


def start_h_kernel(h_ref, h_out):
    h_half = h_ref[...].astype(bf16)
    for k in range(N_CHIP):
        h_out[k] = h_half


def start_w_kernel(rows, cols, count, w_ref, own_ref, w_out, live_ref, place):
    for g in range(CAP):
        place[0, 0, g] = cols[0, 0, g] * ROW_TILES + rows[0, 0, g]
    slot = lax.broadcasted_iota(jnp.int32, (CAP, TILE), 0)
    live_ref[...] = (slot < count[0, 0]).astype(f32)
    own_ref[:, :RANK] = w_ref[:OWN, :]
    own_ref[:, RANK:] = w_ref[OWN:, :]
    half = own_ref[...].astype(bf16)
    for k in range(N_KMER):
        w_out[k] = half


def unpack(w_ref, tiles_ref):
    for k in range(N_KMER):
        r, q = k // 4, k % 4
        block = w_ref[k]
        tiles_ref[r, 32 * q : 32 * q + OWN, :] = block[:, :RANK]
        tiles_ref[r, 32 * q + OWN : 32 * q + 2 * OWN, :] = block[:, RANK:]


def ratio_of(g, place, live_ref, values_ref, tiles_ref, h_ref):
    r, c = place[0, 0, g] & (ROW_TILES - 1), place[0, 0, g] >> 2
    h_tile = h_ref[c & 1, c >> 1]
    estimate = jnp.dot(tiles_ref[r], h_tile, preferred_element_type=f32)
    ratio = values_ref[g].astype(f32) / estimate
    ratio = jnp.where(live_ref[g : g + 1, :] > 0.0, ratio, 0.0).astype(bf16)
    return r, c, h_tile, ratio


def numer_h_kernel(place, live_ref, values_ref, w_ref, h_ref, out_ref, tiles_ref, flip_ref):
    own_core = lax.axis_index("samp") & 1
    unpack(w_ref, tiles_ref)
    for r in range(ROW_TILES):
        flip_ref[r] = tiles_ref[r].T
    sums = jnp.sum(w_ref[...].astype(f32).reshape(N_KMER * OWN, 2 * RANK), axis=0, keepdims=True)
    out_ref[:, :, :RANK, :] = jnp.zeros((2, N_CHIP, RANK, TILE), f32)
    out_ref[:, :, RANK:, :] = jnp.broadcast_to(sums[None, None], (2, N_CHIP, SUMS, TILE))
    for g in range(CAP):
        r, c, h_tile, ratio = ratio_of(g, place, live_ref, values_ref, tiles_ref, h_ref)
        out_ref[jnp.bitwise_xor(c & 1, own_core), c >> 1, :RANK, :] += jnp.dot(flip_ref[r], ratio, preferred_element_type=f32)


def update_h_kernel(parts_ref, h_ref, own_ref, out_ref):
    summed = parts_ref[0]
    for k in range(1, N_CHIP):
        summed = summed + parts_ref[k]
    total = jnp.where(same_rank((RANK, TILE)), summed[RANK : RANK + 1], 0.0)
    h_new = h_ref[...] * summed[:RANK] / jnp.sum(total, axis=1, keepdims=True)
    own_ref[...] = h_new
    half = h_new.astype(bf16)
    for k in range(N_CHIP):
        out_ref[k] = half


def numer_w_kernel(place, live_ref, values_ref, w_ref, h_ref, out_ref, tiles_ref, acc_ref):
    unpack(w_ref, tiles_ref)
    sums = jnp.zeros((RANK, TILE), f32)
    for c in range(COL_TILES):
        sums = sums + h_ref[c % 2, c // 2].astype(f32)
    sums = jnp.where(same_rank((RANK, TILE)), jnp.sum(sums, axis=1, keepdims=True), 0.0)
    sums = jnp.sum(sums, axis=0, keepdims=True)
    out_ref[:, QUADS - 1] = jnp.broadcast_to(sums[None], (N_KMER, QUAD, TILE))
    acc_ref[...] = jnp.zeros_like(acc_ref)
    for g in range(CAP):
        r, c, h_tile, ratio = ratio_of(g, place, live_ref, values_ref, tiles_ref, h_ref)
        acc_ref[r] += lax.dot_general(
            ratio, h_tile, (((1,), (1,)), ((), ())), preferred_element_type=f32
        )
    for k in range(N_KMER):
        r, q = k // 4, k % 4
        for a in range(OWN // QUAD):
            row = 32 * q + QUAD * a
            out_ref[k, a, :, :RANK] = acc_ref[r, row : row + QUAD, :]
            out_ref[k, a, :, RANK:] = acc_ref[r, row + OWN : row + OWN + QUAD, :]


def new_w(parts_ref, w_ref, rows_ref):
    summed = parts_ref[0]
    for k in range(1, N_KMER):
        summed = summed + parts_ref[k]
    for a in range(OWN // QUAD):
        rows_ref[QUAD * a : QUAD * a + QUAD, :] = summed[a]
    return w_ref[...] * rows_ref[...] / summed[QUADS - 1, :1]


def update_w_kernel(parts_ref, w_ref, own_ref, out_ref, rows_ref):
    w_new = new_w(parts_ref, w_ref, rows_ref)
    own_ref[...] = w_new
    half = w_new.astype(bf16)
    for k in range(N_KMER):
        out_ref[k] = half


def last_w_kernel(parts_ref, w_ref, own_ref, rows_ref):
    w_new = new_w(parts_ref, w_ref, rows_ref)
    own_ref[:OWN, :] = w_new[:, :RANK]
    own_ref[OWN:, :] = w_new[:, RANK:]


def swap(bits):
    return [(i, i ^ bits) for i in range(2 * N_CHIP)]


def to_kmer(x):
    return lax.all_to_all(x, "kmer", 0, 0)


def to_chips(x):
    return lax.all_to_all(x, "samp", 0, 0, axis_index_groups=CHIPS)


def panel_of(spread):
    return lax.all_gather(to_chips(spread), "samp", axis=0, axis_index_groups=CORES)


def body(tile_rows, tile_cols, tile_count, tile_values, w_init, h_init):
    shape = jax.ShapeDtypeStruct
    values = tile_values.reshape(CAP, TILE, TILE)
    w_spread = shape((N_KMER, OWN, 2 * RANK), bf16)
    h_spread = shape((N_CHIP, RANK, TILE), bf16)
    w_own, h_own = shape((OWN, 2 * RANK), f32), shape((RANK, TILE), f32)
    tiles = pltpu.VMEM((ROW_TILES, TILE, RANK), bf16)
    flip = pltpu.VMEM((ROW_TILES, RANK, TILE), bf16)
    acc = pltpu.VMEM((ROW_TILES, TILE, RANK), f32)
    rows = pltpu.VMEM((OWN, 2 * RANK), f32)
    wide = [SMEM] + [VMEM] * 4

    live = shape((CAP, TILE), f32)
    start_h = call(start_h_kernel, h_spread, [VMEM])
    place = shape((1, 1, CAP), jnp.int32)
    start_w = call(start_w_kernel, (w_own, w_spread, live, place), [SMEM] * 3 + [VMEM])
    numer_h = call(numer_h_kernel, shape((2, N_CHIP, RANK + SUMS, TILE), f32), wide, [tiles, flip])
    update_h = call(update_h_kernel, (h_own, h_spread), [VMEM] * 2)
    numer_w = call(numer_w_kernel, shape((N_KMER, QUADS, QUAD, TILE), f32), wide, [tiles, acc])
    update_w = call(update_w_kernel, (w_own, w_spread), [VMEM] * 2, [rows])
    last_w = call(last_w_kernel, shape((2 * OWN, RANK), f32), [VMEM] * 2, [rows])

    h_out = start_h(h_init)
    w_own, w_out, live, place = start_w(tile_rows, tile_cols, tile_count, w_init)
    slots = (place, live)
    h_own = h_init
    w_panel = to_kmer(w_out)
    h_panel = panel_of(h_out)
    for sweep in range(ITERS):
        numer = numer_h(*slots, values, w_panel, h_panel)
        numer = numer[0] + lax.ppermute(numer[1], "samp", swap(1))
        h_own, h_out = update_h(to_chips(numer), h_own)
        h_panel = panel_of(h_out)
        parts = to_kmer(numer_w(*slots, values, w_panel, h_panel))
        if sweep < ITERS - 1:
            w_own, w_out = update_w(parts, w_own)
            w_panel = to_kmer(w_out)
    return last_w(parts, w_own), h_own


def solution(mesh):
    in_specs = (
        P("samp", "kmer", None),
        P("samp", "kmer", None),
        P("samp", "kmer"),
        P("samp", "kmer", None, None, None),
        P(("samp", "kmer"), None),
        P(None, ("kmer", "samp")),
    )
    out_specs = (P(("samp", "kmer"), None), P(None, ("kmer", "samp")))
    return jax.shard_map(body, mesh=mesh, in_specs=in_specs, out_specs=out_specs, check_vma=False)
```

```python
import jax
import jax.numpy as jnp
from jax import lax
from jax.experimental import pallas as pl
from jax.experimental.pallas import tpu as pltpu
from jax.sharding import PartitionSpec as P

TILE = 128
RANK = 64
ROW_TILES = 4
COL_TILES = 32
CAP = 32
ITERS = 2
N_KMER = 16
N_CHIP = 16
OWN = 16
SUMS = 8
ROWS = OWN + 1

CORES = [[2 * a, 2 * a + 1] for a in range(N_CHIP)]
CHIPS = [[2 * a + c for a in range(N_CHIP)] for c in range(2)]

f32 = jnp.float32
bf16 = jnp.bfloat16
VMEM = pl.BlockSpec(memory_space=pltpu.VMEM)
SMEM = pl.BlockSpec(memory_space=pltpu.SMEM)


def call(kernel, out_shape, in_specs, scratch=(), out_spec=VMEM):
    return pl.pallas_call(
        kernel,
        out_shape=out_shape,
        in_specs=in_specs,
        out_specs=jax.tree.map(lambda x: SMEM if x.dtype == jnp.int32 else out_spec, out_shape),
        scratch_shapes=scratch,
        compiler_params=pltpu.CompilerParams(vmem_limit_bytes=32 * 2**20),
    )


def same_rank(shape):
    rank = lax.broadcasted_iota(jnp.int32, shape, 0)
    lane = lax.broadcasted_iota(jnp.int32, shape, 1)
    return jnp.bitwise_and(lane, RANK - 1) == rank


def start_h_kernel(h_ref, h_out):
    h_half = h_ref[...].astype(bf16)
    for k in range(N_CHIP):
        h_out[k] = h_half


def start_w_kernel(rows, cols, count, w_ref, own_ref, w_out, live_ref, place):
    for g in range(CAP):
        place[0, 0, g] = cols[0, 0, g] * ROW_TILES + rows[0, 0, g]
    slot = lax.broadcasted_iota(jnp.int32, (CAP, TILE), 0)
    live_ref[...] = (slot < count[0, 0]).astype(f32)
    own_ref[:, :RANK] = w_ref[:OWN, :]
    own_ref[:, RANK:] = w_ref[OWN:, :]
    half = own_ref[...].astype(bf16)
    for k in range(N_KMER):
        w_out[k] = half


def unpack(w_ref, tiles_ref):
    for k in range(N_KMER):
        r, q = k // 4, k % 4
        block = w_ref[k]
        tiles_ref[r, 32 * q : 32 * q + OWN, :] = block[:, :RANK]
        tiles_ref[r, 32 * q + OWN : 32 * q + 2 * OWN, :] = block[:, RANK:]


def fetch(place_ref, place, sem):
    copy = pltpu.make_async_copy(place_ref, place, sem)
    copy.start()
    return copy


def ratio_of(g, place, live_ref, values_ref, tiles_ref, h_ref):
    r, c = place[0, 0, g] & (ROW_TILES - 1), place[0, 0, g] >> 2
    h_tile = h_ref[c & 1, c >> 1]
    estimate = jnp.dot(tiles_ref[r], h_tile, preferred_element_type=f32)
    ratio = values_ref[g].astype(f32) / estimate
    ratio = jnp.where(live_ref[g : g + 1, :] > 0.0, ratio, 0.0).astype(bf16)
    return r, c, h_tile, ratio


def numer_h_kernel(place_ref, live_ref, values_ref, w_ref, h_ref, out_ref, place, sem, tiles_ref, flip_ref):
    copy = fetch(place_ref, place, sem)
    own_core = lax.axis_index("samp") & 1
    unpack(w_ref, tiles_ref)
    for r in range(ROW_TILES):
        flip_ref[r] = tiles_ref[r].T
    sums = jnp.sum(w_ref[...].astype(f32).reshape(N_KMER * OWN, 2 * RANK), axis=0, keepdims=True)
    out_ref[:, :, :RANK, :] = jnp.zeros((2, N_CHIP, RANK, TILE), f32)
    out_ref[:, :, RANK:, :] = jnp.broadcast_to(sums[None, None], (2, N_CHIP, SUMS, TILE))
    copy.wait()
    for g in range(CAP):
        r, c, h_tile, ratio = ratio_of(g, place, live_ref, values_ref, tiles_ref, h_ref)
        out_ref[jnp.bitwise_xor(c & 1, own_core), c >> 1, :RANK, :] += jnp.dot(flip_ref[r], ratio, preferred_element_type=f32)


def update_h_kernel(parts_ref, h_ref, own_ref, out_ref):
    summed = parts_ref[0]
    for k in range(1, N_CHIP):
        summed = summed + parts_ref[k]
    total = jnp.where(same_rank((RANK, TILE)), summed[RANK : RANK + 1], 0.0)
    h_new = h_ref[...] * summed[:RANK] / jnp.sum(total, axis=1, keepdims=True)
    own_ref[...] = h_new
    half = h_new.astype(bf16)
    for k in range(N_CHIP):
        out_ref[k] = half


def numer_w_kernel(place_ref, live_ref, values_ref, w_ref, h_ref, out_ref, place, sem, tiles_ref, acc_ref):
    copy = fetch(place_ref, place, sem)
    unpack(w_ref, tiles_ref)
    sums = jnp.zeros((RANK, TILE), f32)
    for c in range(COL_TILES):
        sums = sums + h_ref[c % 2, c // 2].astype(f32)
    sums = jnp.where(same_rank((RANK, TILE)), jnp.sum(sums, axis=1, keepdims=True), 0.0)
    sums = jnp.sum(sums, axis=0, keepdims=True)
    acc_ref[...] = jnp.zeros_like(acc_ref)
    copy.wait()
    for g in range(CAP):
        r, c, h_tile, ratio = ratio_of(g, place, live_ref, values_ref, tiles_ref, h_ref)
        acc_ref[r] += lax.dot_general(
            ratio, h_tile, (((1,), (1,)), ((), ())), preferred_element_type=f32
        )
    for k in range(N_KMER):
        r, q = k // 4, k % 4
        out_ref[k * ROWS : k * ROWS + OWN, :RANK] = acc_ref[r, 32 * q : 32 * q + OWN, :]
        out_ref[k * ROWS : k * ROWS + OWN, RANK:] = acc_ref[r, 32 * q + OWN : 32 * q + 2 * OWN, :]
        out_ref[k * ROWS + OWN : (k + 1) * ROWS, :] = sums


def new_w(parts_ref, w_ref):
    summed = parts_ref[:OWN, :]
    total = parts_ref[OWN:ROWS, :]
    for k in range(1, N_KMER):
        summed = summed + parts_ref[k * ROWS : k * ROWS + OWN, :]
        total = total + parts_ref[k * ROWS + OWN : (k + 1) * ROWS, :]
    return w_ref[...] * summed / total


def update_w_kernel(parts_ref, w_ref, own_ref, out_ref):
    w_new = new_w(parts_ref, w_ref)
    own_ref[...] = w_new
    half = w_new.astype(bf16)
    for k in range(N_KMER):
        out_ref[k] = half


def last_w_kernel(parts_ref, w_ref, h_ref, w_out, h_out, own_ref, sems):
    h_copy = pltpu.make_async_copy(h_ref, h_out, sems.at[0])
    h_copy.start()
    w_new = new_w(parts_ref, w_ref)
    own_ref[:OWN, :] = w_new[:, :RANK]
    own_ref[OWN:, :] = w_new[:, RANK:]
    w_copy = pltpu.make_async_copy(own_ref, w_out, sems.at[1])
    w_copy.start()
    h_copy.wait()
    w_copy.wait()


def swap(bits):
    return [(i, i ^ bits) for i in range(2 * N_CHIP)]


def to_kmer(x):
    return lax.all_to_all(x, "kmer", 0, 0)


def to_chips(x):
    return lax.all_to_all(x, "samp", 0, 0, axis_index_groups=CHIPS)


def panel_of(spread):
    return lax.all_gather(to_chips(spread), "samp", axis=0, axis_index_groups=CORES)


def body(tile_rows, tile_cols, tile_count, tile_values, w_init, h_init):
    shape = jax.ShapeDtypeStruct
    values = tile_values.reshape(CAP, TILE, TILE)
    w_spread = shape((N_KMER, OWN, 2 * RANK), bf16)
    h_spread = shape((N_CHIP, RANK, TILE), bf16)
    w_own, h_own = shape((OWN, 2 * RANK), f32), shape((RANK, TILE), f32)
    tiles = pltpu.VMEM((ROW_TILES, TILE, RANK), bf16)
    flip = pltpu.VMEM((ROW_TILES, RANK, TILE), bf16)
    acc = pltpu.VMEM((ROW_TILES, TILE, RANK), f32)
    wide = [VMEM] * 5
    fetched = [pltpu.SMEM((1, 1, CAP), jnp.int32), pltpu.SemaphoreType.DMA(())]

    live = shape((CAP, TILE), f32)
    start_h = call(start_h_kernel, h_spread, [VMEM])
    place = shape((1, 1, CAP), jnp.int32)
    start_w = call(start_w_kernel, (w_own, w_spread, live, place), [SMEM] * 3 + [VMEM])
    numer_h = call(numer_h_kernel, shape((2, N_CHIP, RANK + SUMS, TILE), f32), wide, fetched + [tiles, flip])
    update_h = call(update_h_kernel, (h_own, h_spread), [VMEM] * 2)
    numer_w = call(numer_w_kernel, shape((N_KMER * ROWS, TILE), f32), wide, fetched + [tiles, acc])
    update_w = call(update_w_kernel, (w_own, w_spread), [VMEM] * 2)
    last_w = call(
        last_w_kernel,
        (shape(w_init.shape, f32), shape(h_init.shape, f32)),
        [VMEM] * 3,
        [pltpu.VMEM(w_init.shape, f32), pltpu.SemaphoreType.DMA((2,))],
        pl.BlockSpec(memory_space=pl.ANY),
    )

    h_out = start_h(h_init)
    w_own, w_out, live, place = start_w(tile_rows, tile_cols, tile_count, w_init)
    slots = (place, live)
    h_own = h_init
    w_panel = to_kmer(w_out)
    h_panel = panel_of(h_out)
    for sweep in range(ITERS):
        numer = numer_h(*slots, values, w_panel, h_panel)
        numer = numer[0] + lax.ppermute(numer[1], "samp", swap(1))
        h_own, h_out = update_h(to_chips(numer), h_own)
        h_panel = panel_of(h_out)
        parts = numer_w(*slots, values, w_panel, h_panel).reshape(N_KMER, ROWS, 1, TILE)
        parts = to_kmer(parts).reshape(N_KMER * ROWS, TILE)
        if sweep < ITERS - 1:
            w_own, w_out = update_w(parts, w_own)
            w_panel = to_kmer(w_out)
    return last_w(parts, w_own, h_own)


def solution(mesh):
    in_specs = (
        P("samp", "kmer", None),
        P("samp", "kmer", None),
        P("samp", "kmer"),
        P("samp", "kmer", None, None, None),
        P(("samp", "kmer"), None),
        P(None, ("kmer", "samp")),
    )
    out_specs = (P(("samp", "kmer"), None), P(None, ("kmer", "samp")))
    return jax.shard_map(body, mesh=mesh, in_specs=in_specs, out_specs=out_specs, check_vma=False)
```

```python
import jax
import jax.numpy as jnp
from jax import lax
from jax.experimental import pallas as pl
from jax.experimental.pallas import tpu as pltpu
from jax.sharding import PartitionSpec as P

TILE = 128
RANK = 64
ROW_TILES = 4
COL_TILES = 32
CAP = 32
ITERS = 2
N_KMER = 16
N_CHIP = 16
OWN = 16
WIDE = RANK + 1
AHEAD = (6, 12)
ROWS = OWN + 1

CORES = [[2 * a, 2 * a + 1] for a in range(N_CHIP)]
CHIPS = [[2 * a + c for a in range(N_CHIP)] for c in range(2)]

f32 = jnp.float32
bf16 = jnp.bfloat16
VMEM = pl.BlockSpec(memory_space=pltpu.VMEM)
SMEM = pl.BlockSpec(memory_space=pltpu.SMEM)


def call(kernel, out_shape, in_specs, scratch=(), out_spec=VMEM):
    return pl.pallas_call(
        kernel,
        out_shape=out_shape,
        in_specs=in_specs,
        out_specs=jax.tree.map(lambda x: SMEM if x.dtype == jnp.int32 else out_spec, out_shape),
        scratch_shapes=scratch,
        compiler_params=pltpu.CompilerParams(vmem_limit_bytes=32 * 2**20),
    )


def same_rank(shape):
    rank = lax.broadcasted_iota(jnp.int32, shape, 0)
    lane = lax.broadcasted_iota(jnp.int32, shape, 1)
    return jnp.bitwise_and(lane, RANK - 1) == rank


def start_h_kernel(h_ref, h_out):
    h_half = h_ref[...].astype(bf16)
    for k in range(N_CHIP):
        h_out[k] = h_half


def start_w_kernel(rows, cols, count, w_ref, own_ref, w_out, live_ref, place):
    for g in range(CAP):
        place[0, 0, g] = cols[0, 0, g] * ROW_TILES + rows[0, 0, g]
    slot = lax.broadcasted_iota(jnp.int32, (CAP, TILE), 0)
    live_ref[...] = (slot < count[0, 0]).astype(f32)
    own_ref[:, :RANK] = w_ref[:OWN, :]
    own_ref[:, RANK:] = w_ref[OWN:, :]
    half = own_ref[...].astype(bf16)
    for k in range(N_KMER):
        w_out[k] = half


def unpack(w_ref, tiles_ref):
    for k in range(N_KMER):
        r, q = k // 4, k % 4
        block = w_ref[k]
        tiles_ref[r, 32 * q : 32 * q + OWN, :] = block[:, :RANK]
        tiles_ref[r, 32 * q + OWN : 32 * q + 2 * OWN, :] = block[:, RANK:]


def fetch(place_ref, place, sem):
    copy = pltpu.make_async_copy(place_ref, place, sem)
    copy.start()
    return copy


def place_of(place, g):
    return place[0, 0, g] & (ROW_TILES - 1), place[0, 0, g] >> 2


def estimate_of(r, c, tiles_ref, h_ref):
    return jnp.dot(tiles_ref[r], h_ref[c & 1, c >> 1], preferred_element_type=f32)


def ratio_of(g, estimate, live_ref, values_ref):
    ratio = values_ref[g].astype(f32) / estimate
    return jnp.where(live_ref[g : g + 1, :] > 0.0, ratio, 0.0).astype(bf16)


def numer_h_kernel(place_ref, live_ref, values_ref, w_ref, h_ref, out_ref, place, sem, tiles_ref, flip_ref, acc_ref):
    copy = fetch(place_ref, place, sem)
    own_core = lax.axis_index("samp") & 1
    unpack(w_ref, tiles_ref)
    for r in range(ROW_TILES):
        flip_ref[r] = tiles_ref[r].T
    sums = jnp.sum(w_ref[...].astype(f32).reshape(N_KMER * OWN, 2 * RANK), axis=0, keepdims=True)
    acc_ref[...] = jnp.zeros_like(acc_ref)
    copy.wait()
    places = [place_of(place, g) for g in range(CAP)]
    estimates, ratios = {}, {}
    for step in range(CAP + sum(AHEAD)):
        if step < CAP:
            estimates[step] = estimate_of(*places[step], tiles_ref, h_ref)
        g = step - AHEAD[0]
        if 0 <= g < CAP:
            ratios[g] = ratio_of(g, estimates.pop(g), live_ref, values_ref)
        g = g - AHEAD[1]
        if 0 <= g < CAP:
            r, c = places[g]
            term = jnp.dot(flip_ref[r], ratios.pop(g), preferred_element_type=f32)
            acc_ref[jnp.bitwise_xor(c & 1, own_core), c >> 1] += term
    for half in range(2):
        for k in range(N_CHIP):
            out_ref[half, k * WIDE : k * WIDE + RANK, :] = acc_ref[half, k]
            out_ref[half, k * WIDE + RANK : (k + 1) * WIDE, :] = sums


def update_h_kernel(parts_ref, h_ref, own_ref, out_ref):
    summed = parts_ref[:RANK, :]
    total = parts_ref[RANK:WIDE, :]
    for k in range(1, N_CHIP):
        summed = summed + parts_ref[k * WIDE : k * WIDE + RANK, :]
        total = total + parts_ref[k * WIDE + RANK : (k + 1) * WIDE, :]
    total = jnp.where(same_rank((RANK, TILE)), total, 0.0)
    h_new = h_ref[...] * summed / jnp.sum(total, axis=1, keepdims=True)
    own_ref[...] = h_new
    half = h_new.astype(bf16)
    for k in range(N_CHIP):
        out_ref[k] = half


def numer_w_kernel(place_ref, live_ref, values_ref, w_ref, h_ref, out_ref, place, sem, tiles_ref, acc_ref):
    copy = fetch(place_ref, place, sem)
    unpack(w_ref, tiles_ref)
    sums = jnp.zeros((RANK, TILE), f32)
    for c in range(COL_TILES):
        sums = sums + h_ref[c % 2, c // 2].astype(f32)
    sums = jnp.where(same_rank((RANK, TILE)), jnp.sum(sums, axis=1, keepdims=True), 0.0)
    sums = jnp.sum(sums, axis=0, keepdims=True)
    acc_ref[...] = jnp.zeros_like(acc_ref)
    copy.wait()
    for g in range(CAP):
        r, c = place_of(place, g)
        ratio = ratio_of(g, estimate_of(r, c, tiles_ref, h_ref), live_ref, values_ref)
        acc_ref[r] += lax.dot_general(
            ratio, h_ref[c & 1, c >> 1], (((1,), (1,)), ((), ())), preferred_element_type=f32
        )
    for k in range(N_KMER):
        r, q = k // 4, k % 4
        out_ref[k * ROWS : k * ROWS + OWN, :RANK] = acc_ref[r, 32 * q : 32 * q + OWN, :]
        out_ref[k * ROWS : k * ROWS + OWN, RANK:] = acc_ref[r, 32 * q + OWN : 32 * q + 2 * OWN, :]
        out_ref[k * ROWS + OWN : (k + 1) * ROWS, :] = sums


def new_w(parts_ref, w_ref):
    summed = parts_ref[:OWN, :]
    total = parts_ref[OWN:ROWS, :]
    for k in range(1, N_KMER):
        summed = summed + parts_ref[k * ROWS : k * ROWS + OWN, :]
        total = total + parts_ref[k * ROWS + OWN : (k + 1) * ROWS, :]
    return w_ref[...] * summed / total


def update_w_kernel(parts_ref, w_ref, own_ref, out_ref):
    w_new = new_w(parts_ref, w_ref)
    own_ref[...] = w_new
    half = w_new.astype(bf16)
    for k in range(N_KMER):
        out_ref[k] = half


def last_w_kernel(parts_ref, w_ref, h_ref, w_out, h_out, own_ref, sems):
    h_copy = pltpu.make_async_copy(h_ref, h_out, sems.at[0])
    h_copy.start()
    w_new = new_w(parts_ref, w_ref)
    own_ref[:OWN, :] = w_new[:, :RANK]
    own_ref[OWN:, :] = w_new[:, RANK:]
    w_copy = pltpu.make_async_copy(own_ref, w_out, sems.at[1])
    w_copy.start()
    h_copy.wait()
    w_copy.wait()


def swap(bits):
    return [(i, i ^ bits) for i in range(2 * N_CHIP)]


def to_kmer(x):
    return lax.all_to_all(x, "kmer", 0, 0)


def to_chips(x):
    return lax.all_to_all(x, "samp", 0, 0, axis_index_groups=CHIPS)


def panel_of(spread):
    return lax.all_gather(to_chips(spread), "samp", axis=0, axis_index_groups=CORES)


def body(tile_rows, tile_cols, tile_count, tile_values, w_init, h_init):
    shape = jax.ShapeDtypeStruct
    values = tile_values.reshape(CAP, TILE, TILE)
    w_spread = shape((N_KMER, OWN, 2 * RANK), bf16)
    h_spread = shape((N_CHIP, RANK, TILE), bf16)
    w_own, h_own = shape((OWN, 2 * RANK), f32), shape((RANK, TILE), f32)
    tiles = pltpu.VMEM((ROW_TILES, TILE, RANK), bf16)
    flip = pltpu.VMEM((ROW_TILES, RANK, TILE), bf16)
    halves = pltpu.VMEM((2, N_CHIP, RANK, TILE), f32)
    acc = pltpu.VMEM((ROW_TILES, TILE, RANK), f32)
    wide = [VMEM] * 5
    fetched = [pltpu.SMEM((1, 1, CAP), jnp.int32), pltpu.SemaphoreType.DMA(())]

    live = shape((CAP, TILE), f32)
    start_h = call(start_h_kernel, h_spread, [VMEM])
    place = shape((1, 1, CAP), jnp.int32)
    start_w = call(start_w_kernel, (w_own, w_spread, live, place), [SMEM] * 3 + [VMEM])
    numer_h = call(numer_h_kernel, shape((2, N_CHIP * WIDE, TILE), f32), wide, fetched + [tiles, flip, halves])
    update_h = call(update_h_kernel, (h_own, h_spread), [VMEM] * 2)
    numer_w = call(numer_w_kernel, shape((N_KMER * ROWS, TILE), f32), wide, fetched + [tiles, acc])
    update_w = call(update_w_kernel, (w_own, w_spread), [VMEM] * 2)
    last_w = call(
        last_w_kernel,
        (shape(w_init.shape, f32), shape(h_init.shape, f32)),
        [VMEM] * 3,
        [pltpu.VMEM(w_init.shape, f32), pltpu.SemaphoreType.DMA((2,))],
        pl.BlockSpec(memory_space=pl.ANY),
    )

    h_out = start_h(h_init)
    w_own, w_out, live, place = start_w(tile_rows, tile_cols, tile_count, w_init)
    slots = (place, live)
    h_own = h_init
    w_panel = to_kmer(w_out)
    h_panel = panel_of(h_out)
    for sweep in range(ITERS):
        numer = numer_h(*slots, values, w_panel, h_panel)
        numer = numer[0] + lax.ppermute(numer[1], "samp", swap(1))
        parts = to_chips(numer.reshape(N_CHIP, WIDE, 1, TILE)).reshape(N_CHIP * WIDE, TILE)
        h_own, h_out = update_h(parts, h_own)
        h_panel = panel_of(h_out)
        parts = numer_w(*slots, values, w_panel, h_panel).reshape(N_KMER, ROWS, 1, TILE)
        parts = to_kmer(parts).reshape(N_KMER * ROWS, TILE)
        if sweep < ITERS - 1:
            w_own, w_out = update_w(parts, w_own)
            w_panel = to_kmer(w_out)
    return last_w(parts, w_own, h_own)


def solution(mesh):
    in_specs = (
        P("samp", "kmer", None),
        P("samp", "kmer", None),
        P("samp", "kmer"),
        P("samp", "kmer", None, None, None),
        P(("samp", "kmer"), None),
        P(None, ("kmer", "samp")),
    )
    out_specs = (P(("samp", "kmer"), None), P(None, ("kmer", "samp")))
    return jax.shard_map(body, mesh=mesh, in_specs=in_specs, out_specs=out_specs, check_vma=False)
```

```python
import jax
import jax.numpy as jnp
from jax import lax
from jax.experimental import pallas as pl
from jax.experimental.pallas import tpu as pltpu
from jax.sharding import PartitionSpec as P

TILE = 128
RANK = 64
ROW_TILES = 4
COL_TILES = 32
CAP = 32
ITERS = 2
N_KMER = 16
N_CHIP = 16
OWN = 16
WIDE = RANK + 1
AHEAD = (6, 12)
ROWS = OWN + 1

CORES = [[2 * a, 2 * a + 1] for a in range(N_CHIP)]
CHIPS = [[2 * a + c for a in range(N_CHIP)] for c in range(2)]

f32 = jnp.float32
bf16 = jnp.bfloat16
VMEM = pl.BlockSpec(memory_space=pltpu.VMEM)


def call(kernel, out_shape, in_specs, scratch=(), out_spec=VMEM):
    return pl.pallas_call(
        kernel,
        out_shape=out_shape,
        in_specs=in_specs,
        out_specs=jax.tree.map(lambda _: out_spec, out_shape),
        scratch_shapes=scratch,
        compiler_params=pltpu.CompilerParams(vmem_limit_bytes=32 * 2**20),
    )


def same_rank(shape):
    rank = lax.broadcasted_iota(jnp.int32, shape, 0)
    lane = lax.broadcasted_iota(jnp.int32, shape, 1)
    return jnp.bitwise_and(lane, RANK - 1) == rank


def start_h_kernel(h_ref, h_out):
    h_half = h_ref[...].astype(bf16)
    for k in range(N_CHIP):
        h_out[k] = h_half


def start_w_kernel(rows, cols, count, w_ref, own_ref, w_out, live_ref, place_ref):
    place_ref[...] = cols[...] * ROW_TILES + rows[...]
    slot = lax.broadcasted_iota(jnp.int32, (CAP, TILE), 0)
    live_ref[...] = (slot < count[...]).astype(f32)
    own_ref[:, :RANK] = w_ref[:OWN, :]
    own_ref[:, RANK:] = w_ref[OWN:, :]
    half = own_ref[...].astype(bf16)
    for k in range(N_KMER):
        w_out[k] = half


def unpack(w_ref, tiles_ref):
    for k in range(N_KMER):
        r, q = k // 4, k % 4
        block = w_ref[k]
        tiles_ref[r, 32 * q : 32 * q + OWN, :] = block[:, :RANK]
        tiles_ref[r, 32 * q + OWN : 32 * q + 2 * OWN, :] = block[:, RANK:]


def places_of(place_ref):
    place = place_ref[0]
    return [(place[0, g] & (ROW_TILES - 1), place[0, g] >> 2) for g in range(CAP)]


def estimate_of(r, c, tiles_ref, h_ref):
    return jnp.dot(tiles_ref[r], h_ref[c & 1, c >> 1], preferred_element_type=f32)


def ratio_of(g, estimate, live_ref, values_ref):
    ratio = values_ref[g].astype(f32) / estimate
    return jnp.where(live_ref[g : g + 1, :] > 0.0, ratio, 0.0).astype(bf16)


def numer_h_kernel(place_ref, live_ref, values_ref, w_ref, h_ref, out_ref, tiles_ref, flip_ref, acc_ref):
    own_core = lax.axis_index("samp") & 1
    unpack(w_ref, tiles_ref)
    for r in range(ROW_TILES):
        flip_ref[r] = tiles_ref[r].T
    sums = jnp.sum(w_ref[...].astype(f32).reshape(N_KMER * OWN, 2 * RANK), axis=0, keepdims=True)
    acc_ref[...] = jnp.zeros_like(acc_ref)
    places = places_of(place_ref)
    estimates, ratios = {}, {}
    for step in range(CAP + sum(AHEAD)):
        if step < CAP:
            estimates[step] = estimate_of(*places[step], tiles_ref, h_ref)
        g = step - AHEAD[0]
        if 0 <= g < CAP:
            ratios[g] = ratio_of(g, estimates.pop(g), live_ref, values_ref)
        g = g - AHEAD[1]
        if 0 <= g < CAP:
            r, c = places[g]
            term = jnp.dot(flip_ref[r], ratios.pop(g), preferred_element_type=f32)
            acc_ref[jnp.bitwise_xor(c & 1, own_core), c >> 1] += term
    for half in range(2):
        for k in range(N_CHIP):
            out_ref[half, k * WIDE : k * WIDE + RANK, :] = acc_ref[half, k]
            out_ref[half, k * WIDE + RANK : (k + 1) * WIDE, :] = sums


def update_h_kernel(parts_ref, h_ref, own_ref, out_ref):
    summed = parts_ref[:RANK, :]
    total = parts_ref[RANK:WIDE, :]
    for k in range(1, N_CHIP):
        summed = summed + parts_ref[k * WIDE : k * WIDE + RANK, :]
        total = total + parts_ref[k * WIDE + RANK : (k + 1) * WIDE, :]
    total = jnp.where(same_rank((RANK, TILE)), total, 0.0)
    h_new = h_ref[...] * summed / jnp.sum(total, axis=1, keepdims=True)
    own_ref[...] = h_new
    half = h_new.astype(bf16)
    for k in range(N_CHIP):
        out_ref[k] = half


def numer_w_kernel(place_ref, live_ref, values_ref, w_ref, h_ref, out_ref, tiles_ref, acc_ref):
    unpack(w_ref, tiles_ref)
    sums = jnp.zeros((RANK, TILE), f32)
    for c in range(COL_TILES):
        sums = sums + h_ref[c % 2, c // 2].astype(f32)
    sums = jnp.where(same_rank((RANK, TILE)), jnp.sum(sums, axis=1, keepdims=True), 0.0)
    sums = jnp.sum(sums, axis=0, keepdims=True)
    acc_ref[...] = jnp.zeros_like(acc_ref)
    for g, (r, c) in enumerate(places_of(place_ref)):
        ratio = ratio_of(g, estimate_of(r, c, tiles_ref, h_ref), live_ref, values_ref)
        acc_ref[r] += lax.dot_general(
            ratio, h_ref[c & 1, c >> 1], (((1,), (1,)), ((), ())), preferred_element_type=f32
        )
    for k in range(N_KMER):
        r, q = k // 4, k % 4
        out_ref[k * ROWS : k * ROWS + OWN, :RANK] = acc_ref[r, 32 * q : 32 * q + OWN, :]
        out_ref[k * ROWS : k * ROWS + OWN, RANK:] = acc_ref[r, 32 * q + OWN : 32 * q + 2 * OWN, :]
        out_ref[k * ROWS + OWN : (k + 1) * ROWS, :] = sums


def new_w(parts_ref, w_ref):
    summed = parts_ref[:OWN, :]
    total = parts_ref[OWN:ROWS, :]
    for k in range(1, N_KMER):
        summed = summed + parts_ref[k * ROWS : k * ROWS + OWN, :]
        total = total + parts_ref[k * ROWS + OWN : (k + 1) * ROWS, :]
    return w_ref[...] * summed / total


def update_w_kernel(parts_ref, w_ref, own_ref, out_ref):
    w_new = new_w(parts_ref, w_ref)
    own_ref[...] = w_new
    half = w_new.astype(bf16)
    for k in range(N_KMER):
        out_ref[k] = half


def last_w_kernel(parts_ref, w_ref, h_ref, w_out, h_out, own_ref, sems):
    h_copy = pltpu.make_async_copy(h_ref, h_out, sems.at[0])
    h_copy.start()
    w_new = new_w(parts_ref, w_ref)
    own_ref[:OWN, :] = w_new[:, :RANK]
    own_ref[OWN:, :] = w_new[:, RANK:]
    w_copy = pltpu.make_async_copy(own_ref, w_out, sems.at[1])
    w_copy.start()
    h_copy.wait()
    w_copy.wait()


def swap(bits):
    return [(i, i ^ bits) for i in range(2 * N_CHIP)]


def to_kmer(x):
    return lax.all_to_all(x, "kmer", 0, 0)


def to_chips(x):
    return lax.all_to_all(x, "samp", 0, 0, axis_index_groups=CHIPS)


def panel_of(spread):
    return lax.all_gather(to_chips(spread), "samp", axis=0, axis_index_groups=CORES)


def body(tile_rows, tile_cols, tile_count, tile_values, w_init, h_init):
    shape = jax.ShapeDtypeStruct
    values = tile_values.reshape(CAP, TILE, TILE)
    w_spread = shape((N_KMER, OWN, 2 * RANK), bf16)
    h_spread = shape((N_CHIP, RANK, TILE), bf16)
    w_own, h_own = shape((OWN, 2 * RANK), f32), shape((RANK, TILE), f32)
    tiles = pltpu.VMEM((ROW_TILES, TILE, RANK), bf16)
    flip = pltpu.VMEM((ROW_TILES, RANK, TILE), bf16)
    halves = pltpu.VMEM((2, N_CHIP, RANK, TILE), f32)
    acc = pltpu.VMEM((ROW_TILES, TILE, RANK), f32)
    wide = [VMEM] * 5

    live = shape((CAP, TILE), f32)
    start_h = call(start_h_kernel, h_spread, [VMEM])
    place = shape((1, 1, CAP), jnp.int32)
    start_w = call(start_w_kernel, (w_own, w_spread, live, place), [VMEM] * 4)
    numer_h = call(numer_h_kernel, shape((2, N_CHIP * WIDE, TILE), f32), wide, [tiles, flip, halves])
    update_h = call(update_h_kernel, (h_own, h_spread), [VMEM] * 2)
    numer_w = call(numer_w_kernel, shape((N_KMER * ROWS, TILE), f32), wide, [tiles, acc])
    update_w = call(update_w_kernel, (w_own, w_spread), [VMEM] * 2)
    last_w = call(
        last_w_kernel,
        (shape(w_init.shape, f32), shape(h_init.shape, f32)),
        [VMEM] * 3,
        [pltpu.VMEM(w_init.shape, f32), pltpu.SemaphoreType.DMA((2,))],
        pl.BlockSpec(memory_space=pl.ANY),
    )

    h_out = start_h(h_init)
    w_own, w_out, live, place = start_w(tile_rows, tile_cols, tile_count, w_init)
    slots = (place, live)
    h_own = h_init
    w_panel = to_kmer(w_out)
    h_panel = panel_of(h_out)
    for sweep in range(ITERS):
        numer = numer_h(*slots, values, w_panel, h_panel)
        numer = numer[0] + lax.ppermute(numer[1], "samp", swap(1))
        parts = to_chips(numer.reshape(N_CHIP, WIDE, 1, TILE)).reshape(N_CHIP * WIDE, TILE)
        h_own, h_out = update_h(parts, h_own)
        h_panel = panel_of(h_out)
        parts = numer_w(*slots, values, w_panel, h_panel).reshape(N_KMER, ROWS, 1, TILE)
        parts = to_kmer(parts).reshape(N_KMER * ROWS, TILE)
        if sweep < ITERS - 1:
            w_own, w_out = update_w(parts, w_own)
            w_panel = to_kmer(w_out)
    return last_w(parts, w_own, h_own)


def solution(mesh):
    in_specs = (
        P("samp", "kmer", None),
        P("samp", "kmer", None),
        P("samp", "kmer"),
        P("samp", "kmer", None, None, None),
        P(("samp", "kmer"), None),
        P(None, ("kmer", "samp")),
    )
    out_specs = (P(("samp", "kmer"), None), P(None, ("kmer", "samp")))
    return jax.shard_map(body, mesh=mesh, in_specs=in_specs, out_specs=out_specs, check_vma=False)
```

```python
import jax
import jax.numpy as jnp
from jax import lax
from jax.experimental import pallas as pl
from jax.experimental.pallas import tpu as pltpu
from jax.sharding import PartitionSpec as P

TILE = 128
RANK = 64
ROW_TILES = 4
COL_TILES = 32
CAP = 32
ITERS = 2
N_KMER = 16
N_CHIP = 16
OWN = 16
WIDE = RANK + 1
AHEAD = (6, 12)
ROWS = OWN + 1

CORES = [[2 * a, 2 * a + 1] for a in range(N_CHIP)]
CHIPS = [[2 * a + c for a in range(N_CHIP)] for c in range(2)]

f32 = jnp.float32
bf16 = jnp.bfloat16
VMEM = pl.BlockSpec(memory_space=pltpu.VMEM)


def call(kernel, out_shape, in_specs, scratch=(), out_spec=VMEM):
    return pl.pallas_call(
        kernel,
        out_shape=out_shape,
        in_specs=in_specs,
        out_specs=jax.tree.map(lambda _: out_spec, out_shape),
        scratch_shapes=scratch,
        compiler_params=pltpu.CompilerParams(vmem_limit_bytes=32 * 2**20),
    )


def same_rank(shape):
    rank = lax.broadcasted_iota(jnp.int32, shape, 0)
    lane = lax.broadcasted_iota(jnp.int32, shape, 1)
    return jnp.bitwise_and(lane, RANK - 1) == rank


def start_h_kernel(h_ref, h_out):
    h_half = h_ref[...].astype(bf16)
    for k in range(N_CHIP):
        h_out[k] = h_half


def start_w_kernel(rows, cols, count, w_ref, own_ref, w_out, live_ref, place_ref):
    place_ref[...] = cols[...] * ROW_TILES + rows[...]
    slot = lax.broadcasted_iota(jnp.int32, (CAP, TILE), 0)
    live_ref[...] = (slot < count[...]).astype(f32)
    own_ref[:, :RANK] = w_ref[:OWN, :]
    own_ref[:, RANK:] = w_ref[OWN:, :]
    half = own_ref[...].astype(bf16)
    for k in range(N_KMER):
        w_out[k] = half


def unpack(w_ref, tiles_ref):
    for k in range(N_KMER):
        r, q = k // 4, k % 4
        block = w_ref[k]
        tiles_ref[r, 32 * q : 32 * q + OWN, :] = block[:, :RANK]
        tiles_ref[r, 32 * q + OWN : 32 * q + 2 * OWN, :] = block[:, RANK:]


def places_of(place_ref):
    place = place_ref[0]
    return [(place[0, g] & (ROW_TILES - 1), place[0, g] >> 2) for g in range(CAP)]


def estimate_of(r, c, tiles_ref, h_ref):
    return jnp.dot(tiles_ref[r], h_ref[c & 1, c >> 1], preferred_element_type=f32)


def ratio_of(g, estimate, live_ref, values_ref):
    ratio = values_ref[g].astype(f32) / estimate
    return jnp.where(live_ref[g : g + 1, :] > 0.0, ratio, 0.0).astype(bf16)


def numer_h_kernel(place_ref, live_ref, values_ref, w_ref, h_ref, own_ref, other_ref, tiles_ref, flip_ref, acc_ref):
    own_core = lax.axis_index("samp") & 1
    unpack(w_ref, tiles_ref)
    for r in range(ROW_TILES):
        flip_ref[r] = tiles_ref[r].T
    sums = jnp.sum(w_ref[...].astype(f32).reshape(N_KMER * OWN, 2 * RANK), axis=0, keepdims=True)
    acc_ref[...] = jnp.zeros_like(acc_ref)
    places = places_of(place_ref)
    estimates, ratios = {}, {}
    for step in range(CAP + sum(AHEAD)):
        if step < CAP:
            estimates[step] = estimate_of(*places[step], tiles_ref, h_ref)
        g = step - AHEAD[0]
        if 0 <= g < CAP:
            ratios[g] = ratio_of(g, estimates.pop(g), live_ref, values_ref)
        g = g - AHEAD[1]
        if 0 <= g < CAP:
            r, c = places[g]
            term = jnp.dot(flip_ref[r], ratios.pop(g), preferred_element_type=f32)
            acc_ref[jnp.bitwise_xor(c & 1, own_core), c >> 1] += term
    for half, out_ref in enumerate((own_ref, other_ref)):
        for k in range(N_CHIP):
            out_ref[k * WIDE : k * WIDE + RANK, :] = acc_ref[half, k]
            out_ref[k * WIDE + RANK : (k + 1) * WIDE, :] = sums


def update_h_kernel(parts_ref, h_ref, own_ref, out_ref):
    summed = parts_ref[:RANK, :]
    total = parts_ref[RANK:WIDE, :]
    for k in range(1, N_CHIP):
        summed = summed + parts_ref[k * WIDE : k * WIDE + RANK, :]
        total = total + parts_ref[k * WIDE + RANK : (k + 1) * WIDE, :]
    total = jnp.where(same_rank((RANK, TILE)), total, 0.0)
    h_new = h_ref[...] * summed / jnp.sum(total, axis=1, keepdims=True)
    own_ref[...] = h_new
    half = h_new.astype(bf16)
    for k in range(N_CHIP):
        out_ref[k] = half


def numer_w_kernel(place_ref, live_ref, values_ref, w_ref, h_ref, out_ref, tiles_ref, acc_ref):
    unpack(w_ref, tiles_ref)
    sums = jnp.zeros((RANK, TILE), f32)
    for c in range(COL_TILES):
        sums = sums + h_ref[c % 2, c // 2].astype(f32)
    sums = jnp.where(same_rank((RANK, TILE)), jnp.sum(sums, axis=1, keepdims=True), 0.0)
    sums = jnp.sum(sums, axis=0, keepdims=True)
    acc_ref[...] = jnp.zeros_like(acc_ref)
    for g, (r, c) in enumerate(places_of(place_ref)):
        ratio = ratio_of(g, estimate_of(r, c, tiles_ref, h_ref), live_ref, values_ref)
        acc_ref[r] += lax.dot_general(
            ratio, h_ref[c & 1, c >> 1], (((1,), (1,)), ((), ())), preferred_element_type=f32
        )
    for k in range(N_KMER):
        r, q = k // 4, k % 4
        out_ref[k * ROWS : k * ROWS + OWN, :RANK] = acc_ref[r, 32 * q : 32 * q + OWN, :]
        out_ref[k * ROWS : k * ROWS + OWN, RANK:] = acc_ref[r, 32 * q + OWN : 32 * q + 2 * OWN, :]
        out_ref[k * ROWS + OWN : (k + 1) * ROWS, :] = sums


def new_w(parts_ref, w_ref):
    summed = parts_ref[:OWN, :]
    total = parts_ref[OWN:ROWS, :]
    for k in range(1, N_KMER):
        summed = summed + parts_ref[k * ROWS : k * ROWS + OWN, :]
        total = total + parts_ref[k * ROWS + OWN : (k + 1) * ROWS, :]
    return w_ref[...] * summed / total


def update_w_kernel(parts_ref, w_ref, own_ref, out_ref):
    w_new = new_w(parts_ref, w_ref)
    own_ref[...] = w_new
    half = w_new.astype(bf16)
    for k in range(N_KMER):
        out_ref[k] = half


def last_w_kernel(parts_ref, w_ref, h_ref, w_out, h_out, own_ref, sems):
    h_copy = pltpu.make_async_copy(h_ref, h_out, sems.at[0])
    h_copy.start()
    w_new = new_w(parts_ref, w_ref)
    own_ref[:OWN, :] = w_new[:, :RANK]
    own_ref[OWN:, :] = w_new[:, RANK:]
    w_copy = pltpu.make_async_copy(own_ref, w_out, sems.at[1])
    w_copy.start()
    h_copy.wait()
    w_copy.wait()


def swap(bits):
    return [(i, i ^ bits) for i in range(2 * N_CHIP)]


def to_kmer(x):
    return lax.all_to_all(x, "kmer", 0, 0)


def to_chips(x):
    return lax.all_to_all(x, "samp", 0, 0, axis_index_groups=CHIPS)


def panel_of(spread):
    return lax.all_gather(to_chips(spread), "samp", axis=0, axis_index_groups=CORES)


def body(tile_rows, tile_cols, tile_count, tile_values, w_init, h_init):
    shape = jax.ShapeDtypeStruct
    values = tile_values.reshape(CAP, TILE, TILE)
    w_spread = shape((N_KMER, OWN, 2 * RANK), bf16)
    h_spread = shape((N_CHIP, RANK, TILE), bf16)
    w_own, h_own = shape((OWN, 2 * RANK), f32), shape((RANK, TILE), f32)
    tiles = pltpu.VMEM((ROW_TILES, TILE, RANK), bf16)
    flip = pltpu.VMEM((ROW_TILES, RANK, TILE), bf16)
    halves = pltpu.VMEM((2, N_CHIP, RANK, TILE), f32)
    acc = pltpu.VMEM((ROW_TILES, TILE, RANK), f32)
    wide = [VMEM] * 5

    live = shape((CAP, TILE), f32)
    start_h = call(start_h_kernel, h_spread, [VMEM])
    place = shape((1, 1, CAP), jnp.int32)
    start_w = call(start_w_kernel, (w_own, w_spread, live, place), [VMEM] * 4)
    numer_h = call(numer_h_kernel, (shape((N_CHIP * WIDE, TILE), f32),) * 2, wide, [tiles, flip, halves])
    update_h = call(update_h_kernel, (h_own, h_spread), [VMEM] * 2)
    numer_w = call(numer_w_kernel, shape((N_KMER * ROWS, TILE), f32), wide, [tiles, acc])
    update_w = call(update_w_kernel, (w_own, w_spread), [VMEM] * 2)
    last_w = call(
        last_w_kernel,
        (shape(w_init.shape, f32), shape(h_init.shape, f32)),
        [VMEM] * 3,
        [pltpu.VMEM(w_init.shape, f32), pltpu.SemaphoreType.DMA((2,))],
        pl.BlockSpec(memory_space=pl.ANY),
    )

    h_out = start_h(h_init)
    w_own, w_out, live, place = start_w(tile_rows, tile_cols, tile_count, w_init)
    slots = (place, live)
    h_own = h_init
    w_panel = to_kmer(w_out)
    h_panel = panel_of(h_out)
    for sweep in range(ITERS):
        own, other = numer_h(*slots, values, w_panel, h_panel)
        numer = own + lax.ppermute(other, "samp", swap(1))
        parts = to_chips(numer.reshape(N_CHIP, WIDE, 1, TILE)).reshape(N_CHIP * WIDE, TILE)
        h_own, h_out = update_h(parts, h_own)
        h_panel = panel_of(h_out)
        parts = numer_w(*slots, values, w_panel, h_panel).reshape(N_KMER, ROWS, 1, TILE)
        parts = to_kmer(parts).reshape(N_KMER * ROWS, TILE)
        if sweep < ITERS - 1:
            w_own, w_out = update_w(parts, w_own)
            w_panel = to_kmer(w_out)
    return last_w(parts, w_own, h_own)


def solution(mesh):
    in_specs = (
        P("samp", "kmer", None),
        P("samp", "kmer", None),
        P("samp", "kmer"),
        P("samp", "kmer", None, None, None),
        P(("samp", "kmer"), None),
        P(None, ("kmer", "samp")),
    )
    out_specs = (P(("samp", "kmer"), None), P(None, ("kmer", "samp")))
    return jax.shard_map(body, mesh=mesh, in_specs=in_specs, out_specs=out_specs, check_vma=False)
```
